32 devices in a mesh: groups: 1, ep: 16 (over z, y, x), etp: 2 (over core).
Axes of the slice: x: 2, y: 2, z: 4, core: 2. Of those that a mesh axis runs over, the one named last changes fastest.
Arguments:
- tokens: bfloat16 [2048, 4096], P(('groups', 'ep', 'etp')), may hold values from -6 to 6
- expert_ids: int32 [2048, 8], P(('groups', 'ep', 'etp')), may hold values from 0 to 15, all different within a row; in each aligned block of 64 rows (0 to 63, 64 to 127, ...) at most 40 rows name the same one
- route_weights: float32 [2048, 8], P(('groups', 'ep', 'etp')), may hold values from 0.1 to 1
- gate_proj: bfloat16 [16, 4096, 768], P('ep', None, 'etp'), may hold values from -0.09375 to 0.09375
- up_proj: bfloat16 [16, 4096, 768], P('ep', None, 'etp'), may hold values from -0.09375 to 0.09375
- down_proj: bfloat16 [16, 768, 4096], P('ep', 'etp'), may hold values from -0.21875 to 0.21875
Outputs:
- mixed: bfloat16 [2048, 4096], P(('groups', 'ep', 'etp'))
The draws below stay inside these ranges and needn't reach their ends.
Inputs may be any that keep to these rules, and one draw needn't show every extreme that they name: `expert_ids`: each row names 8 different experts. Within the 64 rows of one device no expert is named by more than 40 rows, and on some device some expert is named by exactly 40 rows.
All inputs are finite; a program needn't handle non-finite values.
Results may differ from the reference program's by a relative error of at most 0.0058.
Values may be sent and summed in bfloat16 or wider, within the bound.
No kernel may reach another device: no remote copies, remote signals or barrier semaphores. Data moves between devices by JAX's collectives and lax.ppermute only.
A program may use at most 128 MiB of HBM per device.

```python
import math
import jax
import jax.numpy as jnp
import numpy as np
from jax import lax

D = 4096
FF = 768
TOPK = 8
TOK_DEV = 64
EXPERTS = 16
TOKENS = 2048
CAP = 40
N_EP = 16
N_ETP = 2


def steps_of(stream_key, dims, cuts, low, top_value):
    gain, own = 1.0, jax.random.fold_in(stream_key, 6)
    for axis_at, blocks in cuts:
        heights = jnp.exp(jax.random.uniform(jax.random.fold_in(own, axis_at), (blocks,), jnp.float32, low / len(cuts), top_value / len(cuts)))
        gain = gain * jnp.repeat(heights, dims[axis_at] // blocks).reshape([-1 if axis == axis_at else 1 for axis in range(len(dims))])
    return gain


def deal_out(stream_key, own, number, rows, count, top, most, lean):
    ranking = jax.random.permutation(stream_key, count)
    packed, usual = portions_of(count, rows * top, most, lean, True), portions_of(count, rows * top, most, lean, False)
    places = jnp.arange(count)

    def named(tallies, rotation):
        used = int((tallies > 0).sum())
        fixed = max(1, used // 4)
        shifted = fixed + (places - fixed + rotation * (used - fixed)) % max(1, count - fixed)
        return jnp.zeros((count,), jnp.int32).at[ranking[jnp.where(places < fixed, places, shifted)]].set(jnp.asarray(tallies, jnp.int32))

    tallies = jnp.where(number % 4 == 0, named(packed, number // 4), named(usual, number - number // 4 - 1))
    mixed = jax.random.permutation(jax.random.fold_in(own, 3), count)
    giver, sink = mixed[0:count // 2 * 2:2], mixed[1:count // 2 * 2:2]
    slack = jnp.minimum(tallies[giver] - 1, most - tallies[sink]) // 2
    slack = jnp.where((giver == ranking[0]) | (sink == ranking[0]) | (tallies[sink] == 0), 0, jnp.maximum(slack, 0))
    shifted = jax.random.randint(jax.random.fold_in(own, 4), (count // 2,), 0, 1 << 20) % (slack + 1)
    tallies = tallies.at[giver].add(-shifted).at[sink].add(shifted)
    items = jnp.searchsorted(jnp.cumsum(tallies), jnp.arange(rows * top), side="right").astype(jnp.int32)
    listing = items.reshape(top, rows).T
    listing = listing[jax.random.permutation(jax.random.fold_in(own, 1), rows)]
    rotation = jax.random.randint(jax.random.fold_in(own, 2), (rows, 1), 0, top)
    return jnp.take_along_axis(listing, (jnp.arange(top)[None, :] + rotation) % top, axis=1)


def portions_of(count, total, bound, lean, full):
    weights = [(1 << 20) // math.isqrt(grade ** lean) + 1 for grade in range(1, count + 1)]
    largest = bound if full else min(bound, max(-(-total // count), total * weights[0] // sum(weights)))
    least = 1 if total - largest >= count - 1 else 0
    counts, surplus = [largest] + [least] * (count - 1), total - largest - least * (count - 1)
    while surplus > 0:
        candidates = [i for i in range(1, count) if counts[i] < largest] or [i for i in range(1, count) if counts[i] < bound]
        pool, left = sum([weights[i] for i in candidates]), surplus
        for i in candidates:
            extra = min(bound - counts[i], max(1, left * weights[i] // pool), surplus)
            counts[i] = counts[i] + extra
            surplus = surplus - extra
    return np.array(counts)


def noise(stream_key, shape, deviation, most, cuts=(), kind=jnp.bfloat16):
    loudness = steps_of(stream_key, shape, cuts, -0.22, 0.18) if cuts else 1.0
    array = jax.random.normal(stream_key, shape, jnp.float32) * deviation * loudness
    return jnp.minimum(jnp.maximum(array, -most), most).astype(kind)


def setup_inputs(seed: int = 0, part: int = 0) -> dict:
    streams_of = jax.random.split(jax.random.key(seed), 7)
    part_keys = jax.random.split(jax.random.fold_in(streams_of[6], part), 7)
    tokens = noise(part_keys[0], (TOKENS, D), 1.0, 6.0, ((0, 32),))
    expert_ids_keys = jax.random.split(jax.random.fold_in(part_keys[1], 1), TOKENS // TOK_DEV)
    expert_ids_turns = jax.random.permutation(jax.random.fold_in(part_keys[1], 3), TOKENS // TOK_DEV)
    expert_ids = jax.vmap(lambda own, number: deal_out(jax.random.fold_in(part_keys[1], 2), own, number, TOK_DEV, EXPERTS, TOPK, CAP, 1))(expert_ids_keys, expert_ids_turns).reshape((TOKENS, TOPK))
    route_weights = jnp.clip(jnp.exp(math.log(1.0) - 2.3025851 * jax.random.uniform(part_keys[2], (TOKENS, TOPK), jnp.float32) ** steps_of(part_keys[2], (TOKENS, TOPK), ((0, 32),), -0.2, 0.2)), 0.1, 1.0)
    gate_proj = noise(streams_of[3], (EXPERTS, D, FF), D ** -0.5, 0.09375, ((0, 16), (2, 2)))
    up_proj = noise(streams_of[4], (EXPERTS, D, FF), D ** -0.5, 0.09375, ((0, 16), (2, 2)))
    down_proj = noise(streams_of[5], (EXPERTS, FF, D), FF ** -0.5, 0.21875, ((0, 16), (1, 2)))
    return dict(tokens=tokens, expert_ids=expert_ids, route_weights=route_weights, gate_proj=gate_proj, up_proj=up_proj, down_proj=down_proj)


def reference(tokens, expert_ids, route_weights, gate_proj, up_proj, down_proj):
    count, top = expert_ids.shape
    width = tokens.shape[1]
    sources = N_EP * N_ETP
    tok_dev = count // sources
    experts = gate_proj.shape[0]
    capacity = max(2, min(tok_dev, tok_dev * top * 5 // (4 * experts)))
    grouped = expert_ids.reshape(sources, tok_dev * top)
    onehot = (grouped[:, :, None] == jnp.arange(experts, dtype=jnp.int32)[None, None, :]).astype(jnp.int32)
    ranks = jnp.cumsum(onehot, axis=1) - onehot
    slots = jnp.sum(ranks * onehot, axis=2).astype(jnp.int32)
    source = jnp.arange(sources, dtype=jnp.int32)[:, None]
    place = ((grouped * sources + source) * capacity + slots).reshape(-1).astype(jnp.int32)
    owner = (jnp.arange(count * top, dtype=jnp.int32) // top).astype(jnp.int32)
    table = jnp.full((experts * sources * capacity,), count, jnp.int32).at[place].set(owner).reshape(experts, -1)
    weight_table = jnp.zeros((experts * sources * capacity,), jnp.float32).at[place].set(
        route_weights.reshape(-1).astype(jnp.float32)).reshape(experts, -1)
    padded = jnp.concatenate([tokens, jnp.zeros((1, width), tokens.dtype)], axis=0)

    def step(total, inputs):
        row_index, row_weight, w_gate, w_up, w_down = inputs
        rows = padded[row_index]
        gate = jnp.dot(rows, w_gate, preferred_element_type=jnp.float32)
        upper = jnp.dot(rows, w_up, preferred_element_type=jnp.float32)
        hidden = (jax.nn.silu(gate) * upper).astype(jnp.bfloat16)
        result = jnp.dot(hidden, w_down, preferred_element_type=jnp.float32).astype(jnp.bfloat16)
        total = total.at[row_index].add(row_weight[:, None] * result.astype(jnp.float32))
        return total, None

    start = jnp.zeros((count + 1, width), jnp.float32)
    total, _ = lax.scan(step, start, (table, weight_table, gate_proj, up_proj, down_proj))
    return total[:count].astype(jnp.bfloat16)
```

```python
import jax
import jax.numpy as jnp
from jax import lax
from jax.sharding import PartitionSpec as P

BF = jnp.bfloat16
F32 = jnp.float32


def on_device(tokens, expert_ids, route_weights, gate_proj, up_proj, down_proj):
    rows, width = tokens.shape
    n_ep = lax.axis_size("ep")
    ring = n_ep // 4
    me = lax.axis_index("ep")
    core = lax.axis_index("etp")
    axes = ("ep", "etp")

    def swap(x):
        return lax.ppermute(x, "etp", [(0, 1), (1, 0)])

    pairs_a = [(2 * i + c, 2 * (i ^ (1, 2)[c]) + c) for i in range(n_ep) for c in range(2)]
    pairs_b = [(2 * i + c, 2 * (i ^ (2, 1)[c]) + c) for i in range(n_ep) for c in range(2)]
    pairs_z = [(i, (i + 4) % n_ep) for i in range(n_ep)]

    def hop_a(x):
        return lax.ppermute(x, axes, pairs_a)

    def hop_b(x):
        return lax.ppermute(x, axes, pairs_b)

    def hop_z(x):
        return lax.ppermute(x, "ep", pairs_z)

    experts = jnp.arange(n_ep, dtype=jnp.int32)
    named = expert_ids[:, :, None] == experts[None, None, :]
    dense = jnp.sum(jnp.where(named, route_weights[:, :, None], 0.0), axis=1)
    everyone = lax.all_gather(dense, "ep", axis=0)
    mine = lax.dynamic_index_in_dim(everyone, me, axis=2, keepdims=False)
    flip_a = jnp.where(core == 0, 1, 2)
    flip_b = 3 - flip_a
    plane = me % 4
    level = me // 4

    groups = []
    block = tokens
    for k in range(ring):
        if k:
            block = hop_z(block)
        a = hop_a(block)
        groups.append((block, a, hop_b(block), hop_b(a)))
    w_gate = jnp.concatenate([gate_proj[0], swap(gate_proj[0])], axis=1)
    w_up = jnp.concatenate([up_proj[0], swap(up_proj[0])], axis=1)
    w_down = jnp.concatenate([down_proj[0], swap(down_proj[0])], axis=0)

    def partial_of(k):
        x = jnp.concatenate(groups[k], axis=0)
        base = ((level - k) % ring) * 4
        source = jnp.stack([base + plane, base + (plane ^ flip_a), base + (plane ^ flip_b), base + (plane ^ 3)])
        scale = mine[source].reshape(4 * rows, 1)
        gate = jnp.dot(x, w_gate, preferred_element_type=F32)
        upper = jnp.dot(x, w_up, preferred_element_type=F32)
        hidden = (jax.nn.silu(gate) * upper).astype(BF)
        result = jnp.dot(hidden, w_down, preferred_element_type=F32)
        return (result * scale).astype(BF).reshape(4, rows, width)

    def add(*terms):
        total = terms[0].astype(F32)
        for term in terms[1:]:
            total = total + term.astype(F32)
        return total.astype(BF)

    carry = None
    for k in list(range(1, ring)) + [0]:
        p = partial_of(k)
        got_b2 = hop_b(p[3])
        got_b1 = hop_b(p[2])
        got_a = hop_a(add(p[1], got_b2))
        terms = [p[0], got_b1, got_a]
        if carry is not None:
            terms.append(hop_z(carry))
        carry = add(*terms)
    return carry


def solution(mesh):
    in_specs = (
        P(("groups", "ep", "etp"), None),
        P(("groups", "ep", "etp"), None),
        P(("groups", "ep", "etp"), None),
        P("ep", None, "etp"),
        P("ep", None, "etp"),
        P("ep", "etp", None),
    )
    out_specs = P(("groups", "ep", "etp"), None)
    return jax.shard_map(
        on_device, mesh=mesh, in_specs=in_specs, out_specs=out_specs, check_vma=False
    )
```

```python
import functools

import jax
import jax.numpy as jnp
from jax import lax
from jax.experimental import pallas as pl
from jax.experimental.pallas import tpu as pltpu
from jax.sharding import PartitionSpec as P

BF = jnp.bfloat16
F32 = jnp.float32
META = 128


def named_by(meta, expert, top):
    ids = meta[:, :top].astype(F32)
    return (ids == expert.astype(F32)).astype(F32)


def weight_for(meta, expert, top):
    m = meta.astype(F32)
    parts = m[:, top : 2 * top] + m[:, 2 * top : 3 * top] + m[:, 3 * top : 4 * top]
    return jnp.sum(named_by(meta, expert, top) * parts, axis=1, keepdims=True)


def one_hot(meta, expert, top, first, slots):
    rows = meta.shape[0]
    named = jnp.sum(named_by(meta, expert, top), axis=1, keepdims=True)
    below = lax.broadcasted_iota(jnp.int32, (rows, rows), 0) > lax.broadcasted_iota(jnp.int32, (rows, rows), 1)
    wide = jnp.broadcast_to(named, (rows, slots)).astype(BF)
    rank = jnp.dot(below.astype(F32).astype(BF), wide, preferred_element_type=F32)
    slot = lax.broadcasted_iota(jnp.int32, (rows, slots), 1).astype(F32)
    hit = jnp.logical_and(rank + float(first) == slot, named > 0.5)
    return hit.astype(F32).astype(BF)


def select_kernel(top, cap, slots, expert_ref, z_ref, a_ref, zm_ref, am_ref, out_ref):
    expert = expert_ref[0]
    dims = (((0,), (0,)), ((), ()))
    pick_z = one_hot(zm_ref[...], expert, top, 0, slots)
    pick_a = one_hot(am_ref[...], expert, top, cap, slots)
    got = lax.dot_general(pick_z, z_ref[...], dims, preferred_element_type=F32)
    got = got + lax.dot_general(pick_a, a_ref[...], dims, preferred_element_type=F32)
    out_ref[...] = got.astype(BF)


def select(expert, z, a, top, cap, slots):
    rows, wide = z.shape
    last = wide // META - 1
    return pl.pallas_call(
        functools.partial(select_kernel, top, cap, slots),
        out_shape=jax.ShapeDtypeStruct((slots, wide), BF),
        grid=(1,),
        in_specs=[
            pl.BlockSpec(memory_space=pltpu.SMEM),
            pl.BlockSpec((rows, wide), lambda i: (0, 0)),
            pl.BlockSpec((rows, wide), lambda i: (0, 0)),
            pl.BlockSpec((rows, META), lambda i: (0, last)),
            pl.BlockSpec((rows, META), lambda i: (0, last)),
        ],
        out_specs=pl.BlockSpec((slots, wide), lambda i: (0, 0)),
        compiler_params=pltpu.CompilerParams(vmem_limit_bytes=16 << 20),
        cost_estimate=pl.CostEstimate(flops=4 * slots * rows * wide, bytes_accessed=6 * rows * wide, transcendentals=0),
    )(expert, z, a, z, a)


def expert_kernel(top, nk, ff, expert_ref, z_ref, a_ref, b_ref, zm_ref, am_ref, bm_ref, w0_ref, w1_ref, d0_ref, d1_ref,
                  pz_ref, pa_ref, pb_ref, acc0, acc1, hid):
    i = pl.program_id(0)
    rows = z_ref.shape[0]

    @pl.when(i == 0)
    def _():
        acc0[...] = jnp.zeros_like(acc0)
        acc1[...] = jnp.zeros_like(acc1)

    @pl.when(i < nk)
    def _():
        x = jnp.concatenate([z_ref[...], a_ref[...], b_ref[...]], axis=0)
        acc0[...] += jnp.dot(x, w0_ref[...], preferred_element_type=F32)
        acc1[...] += jnp.dot(x, w1_ref[...], preferred_element_type=F32)

    @pl.when(i == nk - 1)
    def _():
        for c, acc in enumerate((acc0, acc1)):
            gate = acc[:, :ff]
            hid[:, c * ff : (c + 1) * ff] = (gate / (1.0 + jnp.exp(-gate)) * acc[:, ff:]).astype(BF)

    @pl.when(i >= nk)
    def _():
        expert = expert_ref[0]
        out = jnp.dot(hid[:, :ff], d0_ref[...], preferred_element_type=F32)
        out = out + jnp.dot(hid[:, ff:], d1_ref[...], preferred_element_type=F32)
        pz_ref[...] = (out[:rows] * weight_for(zm_ref[...], expert, top)).astype(BF)
        pa_ref[...] = (out[rows : 2 * rows] * weight_for(am_ref[...], expert, top)).astype(BF)
        pb_ref[...] = (out[2 * rows :] * weight_for(bm_ref[...], expert, top)).astype(BF)


def run_expert(expert, z, a, b, w0, w1, d0, d1, top):
    rows, wide = z.shape
    slots = b.shape[0]
    width = wide - META
    ff = d0.shape[0]
    total = 2 * rows + slots
    last = wide // META - 1
    tile = 1024
    nk = width // tile
    col = lambda i: (0, jnp.minimum(i, nk - 1))
    meta = lambda i: (0, last)
    down = lambda i: (0, jnp.maximum(i - nk, 0))
    return pl.pallas_call(
        functools.partial(expert_kernel, top, nk, ff),
        out_shape=[
            jax.ShapeDtypeStruct((rows, width), BF),
            jax.ShapeDtypeStruct((rows, width), BF),
            jax.ShapeDtypeStruct((slots, width), BF),
        ],
        grid=(2 * nk,),
        in_specs=[
            pl.BlockSpec(memory_space=pltpu.SMEM),
            pl.BlockSpec((rows, tile), col),
            pl.BlockSpec((rows, tile), col),
            pl.BlockSpec((slots, tile), col),
            pl.BlockSpec((rows, META), meta),
            pl.BlockSpec((rows, META), meta),
            pl.BlockSpec((slots, META), meta),
            pl.BlockSpec((tile, 2 * ff), lambda i: (jnp.minimum(i, nk - 1), 0)),
            pl.BlockSpec((tile, 2 * ff), lambda i: (jnp.minimum(i, nk - 1), 0)),
            pl.BlockSpec((ff, tile), down),
            pl.BlockSpec((ff, tile), down),
        ],
        out_specs=[
            pl.BlockSpec((rows, tile), down),
            pl.BlockSpec((rows, tile), down),
            pl.BlockSpec((slots, tile), down),
        ],
        scratch_shapes=[
            pltpu.VMEM((total, 2 * ff), F32),
            pltpu.VMEM((total, 2 * ff), F32),
            pltpu.VMEM((total, 2 * ff), BF),
        ],
        compiler_params=pltpu.CompilerParams(vmem_limit_bytes=32 << 20),
        cost_estimate=pl.CostEstimate(
            flops=12 * total * width * ff, bytes_accessed=12 * ff * width + 4 * total * width, transcendentals=2 * total * ff
        ),
    )(expert, z, a, b, z, a, b, w0, w1, d0, d1)


def put_back_kernel(top, first, slots, n_more, expert_ref, own_ref, meta_ref, got_ref, *refs):
    out_ref = refs[n_more]
    place = one_hot(meta_ref[...], expert_ref[0], top, first, slots)
    total = own_ref[...].astype(F32) + jnp.dot(place, got_ref[...], preferred_element_type=F32)
    for more in refs[:n_more]:
        total = total + more[...].astype(F32)
    out_ref[...] = total.astype(BF)


def put_back(expert, own, block, got, more, top, first):
    rows, width = own.shape
    slots = got.shape[0]
    last = block.shape[1] // META - 1
    whole = lambda i: (0, 0)
    return pl.pallas_call(
        functools.partial(put_back_kernel, top, first, slots, len(more)),
        out_shape=jax.ShapeDtypeStruct((rows, width), BF),
        grid=(1,),
        in_specs=[
            pl.BlockSpec(memory_space=pltpu.SMEM),
            pl.BlockSpec((rows, width), whole),
            pl.BlockSpec((rows, META), lambda i: (0, last)),
            pl.BlockSpec((slots, width), whole),
        ]
        + [pl.BlockSpec((rows, width), whole) for _ in more],
        out_specs=pl.BlockSpec((rows, width), whole),
        compiler_params=pltpu.CompilerParams(vmem_limit_bytes=16 << 20),
        cost_estimate=pl.CostEstimate(
            flops=2 * slots * rows * width, bytes_accessed=(6 + 2 * len(more)) * rows * width, transcendentals=0
        ),
    )(expert, own, block, got, *more)


def on_device(tokens, expert_ids, route_weights, gate_proj, up_proj, down_proj):
    rows, width = tokens.shape
    top = expert_ids.shape[1]
    n_ep = lax.axis_size("ep")
    ring = n_ep // 4
    cap = max(2, min(rows, rows * top * 5 // (4 * n_ep)))
    slots = -(-2 * cap // 16) * 16
    me = lax.axis_index("ep")
    core = lax.axis_index("etp")
    axes = ("ep", "etp")

    pairs_a = [(2 * i + c, 2 * (i ^ (1, 2)[c]) + c) for i in range(n_ep) for c in range(2)]
    pairs_b = [(2 * i + c, 2 * (i ^ (2, 1)[c]) + c) for i in range(n_ep) for c in range(2)]
    pairs_z = [(i, (i + 4) % n_ep) for i in range(n_ep)]

    def hop_a(x):
        return lax.ppermute(x, axes, pairs_a)

    def hop_b(x):
        return lax.ppermute(x, axes, pairs_b)

    def hop_z(x):
        return lax.ppermute(x, "ep", pairs_z)

    def swap(x):
        return lax.ppermute(x, "etp", [(0, 1), (1, 0)])

    mine = me.reshape(1).astype(jnp.int32)
    near = (me ^ jnp.where(core == 0, 2, 1)).reshape(1).astype(jnp.int32)

    high = lax.reduce_precision(route_weights, 8, 7)
    middle = lax.reduce_precision(route_weights - high, 8, 7)
    low = route_weights - high - middle
    meta = jnp.concatenate([expert_ids.astype(F32), high, middle, low], axis=1).astype(BF)
    meta = jnp.pad(meta, ((0, 0), (0, META - meta.shape[1])))
    block = jnp.concatenate([tokens, meta], axis=1)

    blocks = []
    for k in range(ring):
        if k:
            block = hop_z(block)
        a = hop_a(block)
        b = hop_b(select(near, block, a, top, cap, slots))
        blocks.append((block, a, b))

    w0 = jnp.concatenate([gate_proj[0], up_proj[0]], axis=1)
    w1 = swap(w0)
    d0 = down_proj[0]
    d1 = swap(d0)

    parts = [run_expert(mine, z, a, b, w0, w1, d0, d1, top) for z, a, b in blocks]

    carry = None
    for k in list(range(1, ring)) + [0]:
        z, a, _ = blocks[k]
        pz, pa, pb = parts[k]
        got_b = hop_b(pb)
        got_a = hop_a(put_back(near, pa, a, got_b, [], top, cap))
        more = [got_a] if carry is None else [got_a, hop_z(carry)]
        carry = put_back(near, pz, z, got_b, more, top, 0)
    return carry


def solution(mesh):
    in_specs = (
        P(("groups", "ep", "etp"), None),
        P(("groups", "ep", "etp"), None),
        P(("groups", "ep", "etp"), None),
        P("ep", None, "etp"),
        P("ep", None, "etp"),
        P("ep", "etp", None),
    )
    out_specs = P(("groups", "ep", "etp"), None)
    return jax.shard_map(
        on_device, mesh=mesh, in_specs=in_specs, out_specs=out_specs, check_vma=False
    )
```

```python
import functools

import jax
import jax.numpy as jnp
from jax import lax
from jax.experimental import pallas as pl
from jax.experimental.pallas import tpu as pltpu
from jax.sharding import PartitionSpec as P

BF = jnp.bfloat16
F32 = jnp.float32
META = 128


def named_by(meta, expert, top):
    ids = meta[:, :top].astype(F32)
    return (ids == expert.astype(F32)).astype(F32)


def weight_for(meta, expert, top):
    m = meta.astype(F32)
    parts = m[:, top : 2 * top] + m[:, 2 * top : 3 * top] + m[:, 3 * top : 4 * top]
    return jnp.sum(named_by(meta, expert, top) * parts, axis=1, keepdims=True)


def one_hot(meta, expert, top, slots):
    rows = meta.shape[0]
    named = jnp.sum(named_by(meta, expert, top), axis=1, keepdims=True)
    below = lax.broadcasted_iota(jnp.int32, (rows, rows), 0) > lax.broadcasted_iota(jnp.int32, (rows, rows), 1)
    wide = jnp.broadcast_to(named, (rows, slots)).astype(BF)
    rank = jnp.dot(below.astype(F32).astype(BF), wide, preferred_element_type=F32)
    slot = lax.broadcasted_iota(jnp.int32, (rows, slots), 1).astype(F32)
    hit = jnp.logical_and(rank == slot, named > 0.5)
    return hit.astype(F32).astype(BF)


def whole_specs(n):
    return [pl.BlockSpec(memory_space=pltpu.SMEM)] + [pl.BlockSpec(memory_space=pltpu.VMEM)] * n


def select_kernel(top, slots, experts_ref, z_ref, *out_refs):
    width = z_ref.shape[1] - META
    for i, out_ref in enumerate(out_refs):
        pick = one_hot(z_ref[:, width:], experts_ref[1 + i], top, slots)
        rows = lax.dot_general(pick, z_ref[...], (((0,), (0,)), ((), ())), preferred_element_type=F32)
        out_ref[...] = rows.astype(BF)


def select(experts, z, top, slots):
    rows, wide = z.shape
    return pl.pallas_call(
        functools.partial(select_kernel, top, slots),
        out_shape=[jax.ShapeDtypeStruct((slots, wide), BF)] * 3,
        in_specs=whole_specs(1),
        out_specs=[pl.BlockSpec(memory_space=pltpu.VMEM)] * 3,
        compiler_params=pltpu.CompilerParams(vmem_limit_bytes=12 << 20),
        cost_estimate=pl.CostEstimate(flops=6 * slots * rows * wide, bytes_accessed=6 * rows * wide, transcendentals=0),
    )(experts, z)


def prepare_kernel(ids_ref, weights_ref, tokens_ref, out_ref):
    weights = weights_ref[...]
    high = weights.astype(BF).astype(F32)
    middle = (weights - high).astype(BF).astype(F32)
    low = weights - high - middle
    rows, width = tokens_ref.shape
    rest = jnp.zeros((rows, META - 4 * weights.shape[1]), F32)
    meta = jnp.concatenate([ids_ref[...].astype(F32), high, middle, low, rest], axis=1)
    out_ref[:, :width] = tokens_ref[...]
    out_ref[:, width:] = meta.astype(BF)


def prepare(ids, weights, tokens):
    rows, width = tokens.shape
    return pl.pallas_call(
        prepare_kernel,
        out_shape=jax.ShapeDtypeStruct((rows, width + META), BF),
        in_specs=[pl.BlockSpec(memory_space=pltpu.VMEM)] * 3,
        out_specs=pl.BlockSpec(memory_space=pltpu.VMEM),
        compiler_params=pltpu.CompilerParams(vmem_limit_bytes=12 << 20),
        cost_estimate=pl.CostEstimate(flops=rows, bytes_accessed=4 * rows * width, transcendentals=0),
    )(ids, weights, tokens)


def stage_kernel(gate_ref, up_ref, down_ref, joined_ref, held_ref, sems):
    ff = down_ref.shape[0]
    copies = [
        pltpu.make_async_copy(gate_ref, joined_ref.at[:, pl.ds(0, ff)], sems.at[0]),
        pltpu.make_async_copy(up_ref, joined_ref.at[:, pl.ds(ff, ff)], sems.at[1]),
        pltpu.make_async_copy(down_ref, held_ref, sems.at[2]),
    ]
    for copy in copies:
        copy.start()
    for copy in copies:
        copy.wait()


def stage(gate, up, down):
    width, ff = gate.shape
    return pl.pallas_call(
        stage_kernel,
        out_shape=[pltpu.VMEM((width, 2 * ff), BF), pltpu.VMEM(down.shape, BF)],
        in_specs=[pl.BlockSpec(memory_space=pl.ANY)] * 3,
        out_specs=[pl.BlockSpec(memory_space=pltpu.VMEM)] * 2,
        scratch_shapes=[pltpu.SemaphoreType.DMA((3,))],
        compiler_params=pltpu.CompilerParams(vmem_limit_bytes=12 << 20),
        cost_estimate=pl.CostEstimate(flops=width, bytes_accessed=12 * width * ff, transcendentals=0),
    )(gate, up, down)


def expert_kernel(top, pitch, experts_ref, *refs):
    blocks, (w0_ref, d0_ref, w1_ref, d1_ref), outs, (x, hid) = refs[:4], refs[4:8], refs[8:12], refs[12:]
    expert = experts_ref[0]
    rows = blocks[0].shape[0]
    width = w0_ref.shape[0]
    ff = d0_ref.shape[0]
    spans = [(0, rows)] + [(rows + i * pitch, blocks[1].shape[0]) for i in range(3)]
    if pitch > blocks[1].shape[0]:
        x[rows:] = jnp.zeros_like(x[rows:])
    for block, (first, count) in zip(blocks, spans):
        x[first : first + count] = block[:, :width]
    for c, w_ref in enumerate((w0_ref, w1_ref)):
        both = jnp.dot(x[...], w_ref[...], preferred_element_type=F32)
        gate = both[:, :ff]
        hid[:, c * ff : (c + 1) * ff] = (gate / (1.0 + jnp.exp(-gate)) * both[:, ff:]).astype(BF)
    scales = [weight_for(block[:, width:], expert, top) for block in blocks]
    tile = 1024
    for n in range(width // tile):
        s = slice(n * tile, (n + 1) * tile)
        out = jnp.dot(hid[:, :ff], d0_ref[:, s], preferred_element_type=F32)
        out = out + jnp.dot(hid[:, ff:], d1_ref[:, s], preferred_element_type=F32)
        for ref, scale, (first, count) in zip(outs, scales, spans):
            ref[:, s] = (out[first : first + count] * scale).astype(BF)


def run_expert(experts, blocks, weights, top):
    rows, wide = blocks[0].shape
    slots = blocks[1].shape[0]
    width = weights[0].shape[0]
    ff = weights[1].shape[0]
    pitch = -(-slots // 16) * 16
    total = rows + 3 * pitch
    return pl.pallas_call(
        functools.partial(expert_kernel, top, pitch),
        out_shape=[jax.ShapeDtypeStruct((block.shape[0], width), BF) for block in blocks],
        in_specs=whole_specs(8),
        out_specs=[pl.BlockSpec(memory_space=pltpu.VMEM)] * 4,
        scratch_shapes=[pltpu.VMEM((total, width), BF), pltpu.VMEM((total, 2 * ff), BF)],
        compiler_params=pltpu.CompilerParams(vmem_limit_bytes=14 << 20),
        cost_estimate=pl.CostEstimate(
            flops=12 * total * width * ff, bytes_accessed=4 * total * width, transcendentals=2 * total * ff
        ),
    )(experts, *blocks, *weights)


def put_back_kernel(top, slots, n_more, experts_ref, own_ref, block_ref, *refs):
    got, more, out_ref = refs[:3], refs[3 : 3 + n_more], refs[3 + n_more]
    width = own_ref.shape[1]
    total = own_ref[...].astype(F32)
    for i, ref in enumerate(got):
        place = one_hot(block_ref[:, width:], experts_ref[1 + i], top, slots)
        total = total + jnp.dot(place, ref[...], preferred_element_type=F32)
    for ref in more:
        total = total + ref[...].astype(F32)
    out_ref[...] = total.astype(BF)


def put_back(experts, own, block, got, more, top):
    rows, width = own.shape
    slots = got[0].shape[0]
    return pl.pallas_call(
        functools.partial(put_back_kernel, top, slots, len(more)),
        out_shape=jax.ShapeDtypeStruct((rows, width), BF),
        in_specs=whole_specs(5 + len(more)),
        out_specs=pl.BlockSpec(memory_space=pltpu.VMEM),
        compiler_params=pltpu.CompilerParams(vmem_limit_bytes=12 << 20),
        cost_estimate=pl.CostEstimate(
            flops=6 * slots * rows * width, bytes_accessed=(8 + 2 * len(more)) * rows * width, transcendentals=0
        ),
    )(experts, own, block, *got, *more)


def on_device(tokens, expert_ids, route_weights, gate_proj, up_proj, down_proj):
    rows, width = tokens.shape
    top = expert_ids.shape[1]
    n_ep = lax.axis_size("ep")
    ring = n_ep // 4
    cap = max(2, min(rows, rows * top * 5 // (4 * n_ep)))
    slots = -(-cap // 8) * 8
    me = lax.axis_index("ep").astype(jnp.int32)

    def swap(x):
        return lax.ppermute(x, "etp", [(0, 1), (1, 0)])

    def hop_z(x):
        return lax.ppermute(x, "ep", [(i, (i + 4) % n_ep) for i in range(n_ep)])

    def spread(arrays):
        return [
            lax.ppermute(x, "ep", [(i, i ^ flip) for i in range(n_ep)]) for flip, x in zip((1, 2, 3), arrays)
        ]

    def after(x, *others):
        return lax.optimization_barrier((x, *others))[0]

    experts = jnp.stack([me, me ^ 1, me ^ 2, me ^ 3])
    block = prepare(expert_ids, route_weights, tokens)
    half = (gate_proj[0], up_proj[0], down_proj[0])
    other = [swap(x) for x in half]

    levels, given, results, weights = [block], [], [], []

    def compute(k):
        if not weights:
            weights.extend([*stage(*after(half, levels[1])), *stage(*other)])
        mine = after(given[k], results[-1][0]) if results else given[k]
        results.append(run_expert(experts, [levels[k], *mine], weights, top))

    for k in range(ring):
        z = levels[k]
        if k:
            z = levels[k] = after(z, given[k - 1])
        if k > 1:
            compute(k - 2)
        if k + 1 < ring:
            levels.append(hop_z(z))
        given.append(spread(select(experts, z, top, slots)))

    carry = None
    returned = None
    for k in [*range(1, ring), 0]:
        while len(results) < min(ring, k + 2):
            compute(len(results))
        pz, *out = results[k]
        returned = spread(out)
        carry = put_back(experts, pz, levels[k], returned, [] if carry is None else [hop_z(carry)], top)
    return carry
def solution(mesh):
    in_specs = (
        P(("groups", "ep", "etp"), None),
        P(("groups", "ep", "etp"), None),
        P(("groups", "ep", "etp"), None),
        P("ep", None, "etp"),
        P("ep", None, "etp"),
        P("ep", "etp", None),
    )
    out_specs = P(("groups", "ep", "etp"), None)
    return jax.shard_map(
        on_device, mesh=mesh, in_specs=in_specs, out_specs=out_specs, check_vma=False
    )
```

```python
import functools

import jax
import jax.numpy as jnp
from jax import lax
from jax.experimental import pallas as pl
from jax.experimental.pallas import tpu as pltpu
from jax.sharding import PartitionSpec as P

BF = jnp.bfloat16
F32 = jnp.float32
META = 128


def named_by(meta, expert, top):
    ids = meta[:, :top].astype(F32)
    return (ids == expert.astype(F32)).astype(F32)


def weight_for(meta, expert, top):
    m = meta.astype(F32)
    parts = m[:, top : 2 * top] + m[:, 2 * top : 3 * top] + m[:, 3 * top : 4 * top]
    return jnp.sum(named_by(meta, expert, top) * parts, axis=1, keepdims=True)


def one_hot(meta, expert, top, slots):
    rows = meta.shape[0]
    named = jnp.sum(named_by(meta, expert, top), axis=1, keepdims=True)
    below = lax.broadcasted_iota(jnp.int32, (rows, rows), 0) > lax.broadcasted_iota(jnp.int32, (rows, rows), 1)
    wide = jnp.broadcast_to(named, (rows, slots)).astype(BF)
    rank = jnp.dot(below.astype(F32).astype(BF), wide, preferred_element_type=F32)
    slot = lax.broadcasted_iota(jnp.int32, (rows, slots), 1).astype(F32)
    hit = jnp.logical_and(rank == slot, named > 0.5)
    return hit.astype(F32).astype(BF)


def whole_specs(n):
    return [pl.BlockSpec(memory_space=pltpu.SMEM)] + [pl.BlockSpec(memory_space=pltpu.VMEM)] * n


def select_kernel(top, slots, experts_ref, z_ref, *out_refs):
    width = z_ref.shape[1] - META
    for i, out_ref in enumerate(out_refs):
        pick = one_hot(z_ref[:, width:], experts_ref[1 + i], top, slots)
        rows = lax.dot_general(pick, z_ref[...], (((0,), (0,)), ((), ())), preferred_element_type=F32)
        out_ref[...] = rows.astype(BF)


def select(experts, z, top, slots):
    rows, wide = z.shape
    return pl.pallas_call(
        functools.partial(select_kernel, top, slots),
        out_shape=[jax.ShapeDtypeStruct((slots, wide), BF)] * 3,
        in_specs=whole_specs(1),
        out_specs=[pl.BlockSpec(memory_space=pltpu.VMEM)] * 3,
        compiler_params=pltpu.CompilerParams(vmem_limit_bytes=12 << 20),
        cost_estimate=pl.CostEstimate(flops=6 * slots * rows * wide, bytes_accessed=6 * rows * wide, transcendentals=0),
    )(experts, z)


def prepare_kernel(ids_ref, weights_ref, tokens_ref, out_ref):
    weights = weights_ref[...]
    high = weights.astype(BF).astype(F32)
    middle = (weights - high).astype(BF).astype(F32)
    low = weights - high - middle
    rows, width = tokens_ref.shape
    rest = jnp.zeros((rows, META - 4 * weights.shape[1]), F32)
    meta = jnp.concatenate([ids_ref[...].astype(F32), high, middle, low, rest], axis=1)
    out_ref[:, :width] = tokens_ref[...]
    out_ref[:, width:] = meta.astype(BF)


def prepare(ids, weights, tokens):
    rows, width = tokens.shape
    return pl.pallas_call(
        prepare_kernel,
        out_shape=jax.ShapeDtypeStruct((rows, width + META), BF),
        in_specs=[pl.BlockSpec(memory_space=pltpu.VMEM)] * 3,
        out_specs=pl.BlockSpec(memory_space=pltpu.VMEM),
        compiler_params=pltpu.CompilerParams(vmem_limit_bytes=12 << 20),
        cost_estimate=pl.CostEstimate(flops=rows, bytes_accessed=4 * rows * width, transcendentals=0),
    )(ids, weights, tokens)


def stage_kernel(gate_ref, up_ref, down_ref, joined_ref, held_ref, sems):
    ff = down_ref.shape[0]
    copies = [
        pltpu.make_async_copy(gate_ref, joined_ref.at[:, pl.ds(0, ff)], sems.at[0]),
        pltpu.make_async_copy(up_ref, joined_ref.at[:, pl.ds(ff, ff)], sems.at[1]),
        pltpu.make_async_copy(down_ref, held_ref, sems.at[2]),
    ]
    for copy in copies:
        copy.start()
    for copy in copies:
        copy.wait()


def stage(gate, up, down):
    width, ff = gate.shape
    return pl.pallas_call(
        stage_kernel,
        out_shape=[pltpu.VMEM((width, 2 * ff), BF), pltpu.VMEM(down.shape, BF)],
        in_specs=[pl.BlockSpec(memory_space=pl.ANY)] * 3,
        out_specs=[pl.BlockSpec(memory_space=pltpu.VMEM)] * 2,
        scratch_shapes=[pltpu.SemaphoreType.DMA((3,))],
        compiler_params=pltpu.CompilerParams(vmem_limit_bytes=12 << 20),
        cost_estimate=pl.CostEstimate(flops=width, bytes_accessed=12 * width * ff, transcendentals=0),
    )(gate, up, down)


def expert_kernel(top, pitch, experts_ref, *refs):
    blocks, (w0_ref, d0_ref, w1_ref, d1_ref), outs, (x, hid) = refs[:4], refs[4:8], refs[8:12], refs[12:]
    expert = experts_ref[0]
    rows = blocks[0].shape[0]
    width = w0_ref.shape[0]
    ff = d0_ref.shape[0]
    spans = [(0, rows)] + [(rows + i * pitch, blocks[1].shape[0]) for i in range(3)]
    if pitch > blocks[1].shape[0]:
        x[rows:] = jnp.zeros_like(x[rows:])
    for block, (first, count) in zip(blocks, spans):
        x[first : first + count] = block[:, :width]
    for c, w_ref in enumerate((w0_ref, w1_ref)):
        both = jnp.dot(x[...], w_ref[...], preferred_element_type=F32)
        gate = both[:, :ff]
        hid[:, c * ff : (c + 1) * ff] = (gate / (1.0 + jnp.exp(-gate)) * both[:, ff:]).astype(BF)
    scales = [weight_for(block[:, width:], expert, top) for block in blocks]
    tile = 1024
    for n in range(width // tile):
        s = slice(n * tile, (n + 1) * tile)
        out = jnp.dot(hid[:, :ff], d0_ref[:, s], preferred_element_type=F32)
        out = out + jnp.dot(hid[:, ff:], d1_ref[:, s], preferred_element_type=F32)
        for ref, scale, (first, count) in zip(outs, scales, spans):
            ref[:, s] = (out[first : first + count] * scale).astype(BF)


def run_expert(experts, blocks, weights, top):
    rows, wide = blocks[0].shape
    slots = blocks[1].shape[0]
    width = weights[0].shape[0]
    ff = weights[1].shape[0]
    pitch = -(-slots // 16) * 16
    total = rows + 3 * pitch
    return pl.pallas_call(
        functools.partial(expert_kernel, top, pitch),
        out_shape=[jax.ShapeDtypeStruct((block.shape[0], width), BF) for block in blocks],
        in_specs=whole_specs(8),
        out_specs=[pl.BlockSpec(memory_space=pltpu.VMEM)] * 4,
        scratch_shapes=[pltpu.VMEM((total, width), BF), pltpu.VMEM((total, 2 * ff), BF)],
        compiler_params=pltpu.CompilerParams(vmem_limit_bytes=14 << 20),
        cost_estimate=pl.CostEstimate(
            flops=12 * total * width * ff, bytes_accessed=4 * total * width, transcendentals=2 * total * ff
        ),
    )(experts, *blocks, *weights)


def put_back_kernel(top, slots, n_more, experts_ref, own_ref, block_ref, *refs):
    got, more, out_ref = refs[:3], refs[3 : 3 + n_more], refs[3 + n_more]
    width = own_ref.shape[1]
    total = own_ref[...].astype(F32)
    for i, ref in enumerate(got):
        place = one_hot(block_ref[:, width:], experts_ref[1 + i], top, slots)
        total = total + jnp.dot(place, ref[...], preferred_element_type=F32)
    for ref in more:
        total = total + ref[...].astype(F32)
    out_ref[...] = total.astype(BF)


def put_back(experts, own, block, got, more, top):
    rows, width = own.shape
    slots = got[0].shape[0]
    return pl.pallas_call(
        functools.partial(put_back_kernel, top, slots, len(more)),
        out_shape=jax.ShapeDtypeStruct((rows, width), BF),
        in_specs=whole_specs(5 + len(more)),
        out_specs=pl.BlockSpec(memory_space=pltpu.VMEM),
        compiler_params=pltpu.CompilerParams(vmem_limit_bytes=12 << 20),
        cost_estimate=pl.CostEstimate(
            flops=6 * slots * rows * width, bytes_accessed=(8 + 2 * len(more)) * rows * width, transcendentals=0
        ),
    )(experts, own, block, *got, *more)


def on_device(tokens, expert_ids, route_weights, gate_proj, up_proj, down_proj):
    rows, width = tokens.shape
    top = expert_ids.shape[1]
    n_ep = lax.axis_size("ep")
    ring = n_ep // 4
    cap = max(2, min(rows, rows * top * 5 // (4 * n_ep)))
    slots = -(-cap // 8) * 8
    me = lax.axis_index("ep").astype(jnp.int32)

    def swap(x):
        return lax.ppermute(x, "etp", [(0, 1), (1, 0)])

    def hop_z(x):
        return lax.ppermute(x, "ep", [(i, (i + 4) % n_ep) for i in range(n_ep)])

    def spread(arrays):
        return [
            lax.ppermute(x, "ep", [(i, i ^ flip) for i in range(n_ep)]) for flip, x in zip((1, 2, 3), arrays)
        ]

    def after(x, *others):
        return lax.optimization_barrier((x, *others))[0]

    experts = jnp.stack([me, me ^ 1, me ^ 2, me ^ 3])
    block = prepare(expert_ids, route_weights, tokens)
    half = (gate_proj[0], up_proj[0], down_proj[0])
    other = []

    levels, given, results, weights = [block], [], [], []

    def compute(k):
        if not weights:
            other.extend(swap(x) for x in after(half, levels[1]))
            weights.extend([*stage(*after(half, levels[1])), *stage(*other)])
        mine = after(given[k], results[-1][0]) if results else given[k]
        results.append(run_expert(experts, [levels[k], *mine], weights, top))

    for k in range(ring):
        z = levels[k]
        if k:
            z = levels[k] = after(z, given[k - 1])
        if k > 1:
            compute(k - 2)
        if k + 1 < ring:
            levels.append(hop_z(z))
        given.append(spread(select(experts, z, top, slots)))

    carry = None
    returned = None
    for k in [*range(1, ring), 0]:
        while len(results) < min(ring, k + 2):
            compute(len(results))
        pz, *out = results[k]
        returned = spread(out)
        carry = put_back(experts, pz, levels[k], returned, [] if carry is None else [hop_z(carry)], top)
    return carry
def solution(mesh):
    in_specs = (
        P(("groups", "ep", "etp"), None),
        P(("groups", "ep", "etp"), None),
        P(("groups", "ep", "etp"), None),
        P("ep", None, "etp"),
        P("ep", None, "etp"),
        P("ep", "etp", None),
    )
    out_specs = P(("groups", "ep", "etp"), None)
    return jax.shard_map(
        on_device, mesh=mesh, in_specs=in_specs, out_specs=out_specs, check_vma=False
    )
```

```python
import functools

import jax
import jax.numpy as jnp
from jax import lax
from jax.experimental import pallas as pl
from jax.experimental.pallas import tpu as pltpu
from jax.sharding import PartitionSpec as P

BF = jnp.bfloat16
F32 = jnp.float32
META = 128


def named_by(meta, expert, top):
    ids = meta[:, :top].astype(F32)
    return (ids == expert.astype(F32)).astype(F32)


def weight_for(meta, expert, top):
    m = meta.astype(F32)
    parts = m[:, top : 2 * top] + m[:, 2 * top : 3 * top] + m[:, 3 * top : 4 * top]
    return jnp.sum(named_by(meta, expert, top) * parts, axis=1, keepdims=True)


def one_hot(meta, experts_ref, top, slots):
    rows = meta.shape[0]
    ids = meta[:, :top].astype(F32)
    column = lax.broadcasted_iota(jnp.int32, (rows, 3 * slots), 1)
    part = (column >= slots).astype(jnp.int32) + (column >= 2 * slots).astype(jnp.int32)
    expert = jnp.where(part == 0, experts_ref[1], jnp.where(part == 1, experts_ref[2], experts_ref[3])).astype(F32)
    named = jnp.zeros((rows, 3 * slots), F32)
    for k in range(top):
        named = named + (ids[:, k : k + 1] == expert).astype(F32)
    below = lax.broadcasted_iota(jnp.int32, (rows, rows), 0) > lax.broadcasted_iota(jnp.int32, (rows, rows), 1)
    rank = jnp.dot(below.astype(F32).astype(BF), named.astype(BF), preferred_element_type=F32)
    hit = jnp.logical_and(rank == (column - part * slots).astype(F32), named > 0.5)
    return hit.astype(F32).astype(BF)


def whole_specs(n):
    return [pl.BlockSpec(memory_space=pltpu.SMEM)] + [pl.BlockSpec(memory_space=pltpu.VMEM)] * n


def select_kernel(top, slots, experts_ref, z_ref, *out_refs):
    width = z_ref.shape[1] - META
    pick = one_hot(z_ref[:, width:], experts_ref, top, slots)
    rows = lax.dot_general(pick, z_ref[...], (((0,), (0,)), ((), ())), preferred_element_type=F32)
    for i, out_ref in enumerate(out_refs):
        out_ref[...] = rows[i * slots : (i + 1) * slots].astype(BF)


def select(experts, z, top, slots):
    rows, wide = z.shape
    return pl.pallas_call(
        functools.partial(select_kernel, top, slots),
        out_shape=[jax.ShapeDtypeStruct((slots, wide), BF)] * 3,
        in_specs=whole_specs(1),
        out_specs=[pl.BlockSpec(memory_space=pltpu.VMEM)] * 3,
        compiler_params=pltpu.CompilerParams(vmem_limit_bytes=12 << 20),
        cost_estimate=pl.CostEstimate(flops=6 * slots * rows * wide, bytes_accessed=6 * rows * wide, transcendentals=0),
    )(experts, z)


def prepare_kernel(ids_ref, weights_ref, tokens_ref, out_ref):
    weights = weights_ref[...]
    high = weights.astype(BF).astype(F32)
    middle = (weights - high).astype(BF).astype(F32)
    low = weights - high - middle
    rows, width = tokens_ref.shape
    rest = jnp.zeros((META - 4 * weights.shape[0], rows), F32)
    meta = jnp.concatenate([ids_ref[...].astype(F32), high, middle, low, rest], axis=0).T
    out_ref[:, :width] = tokens_ref[...]
    out_ref[:, width:] = meta.astype(BF)


def prepare(ids, weights, tokens):
    rows, width = tokens.shape
    return pl.pallas_call(
        prepare_kernel,
        out_shape=jax.ShapeDtypeStruct((rows, width + META), BF),
        in_specs=[pl.BlockSpec(memory_space=pltpu.VMEM)] * 3,
        out_specs=pl.BlockSpec(memory_space=pltpu.VMEM),
        compiler_params=pltpu.CompilerParams(vmem_limit_bytes=12 << 20),
        cost_estimate=pl.CostEstimate(flops=rows, bytes_accessed=4 * rows * width, transcendentals=0),
    )(ids.T, weights.T, tokens)


def stage_kernel(gate_ref, up_ref, down_ref, joined_ref, held_ref, sems):
    ff = down_ref.shape[0]
    copies = [
        pltpu.make_async_copy(gate_ref, joined_ref.at[:, pl.ds(0, ff)], sems.at[0]),
        pltpu.make_async_copy(up_ref, joined_ref.at[:, pl.ds(ff, ff)], sems.at[1]),
        pltpu.make_async_copy(down_ref, held_ref, sems.at[2]),
    ]
    for copy in copies:
        copy.start()
    for copy in copies:
        copy.wait()


def stage(gate, up, down):
    width, ff = gate.shape
    return pl.pallas_call(
        stage_kernel,
        out_shape=[pltpu.VMEM((width, 2 * ff), BF), pltpu.VMEM(down.shape, BF)],
        in_specs=[pl.BlockSpec(memory_space=pl.ANY)] * 3,
        out_specs=[pl.BlockSpec(memory_space=pltpu.VMEM)] * 2,
        scratch_shapes=[pltpu.SemaphoreType.DMA((3,))],
        compiler_params=pltpu.CompilerParams(vmem_limit_bytes=12 << 20),
        cost_estimate=pl.CostEstimate(flops=width, bytes_accessed=12 * width * ff, transcendentals=0),
    )(gate, up, down)


def expert_kernel(top, pitch, experts_ref, *refs):
    blocks, (w0_ref, d0_ref, w1_ref, d1_ref), outs, (x, hid) = refs[:4], refs[4:8], refs[8:12], refs[12:]
    expert = experts_ref[0]
    rows = blocks[0].shape[0]
    width = w0_ref.shape[0]
    ff = d0_ref.shape[0]
    spans = [(0, rows)] + [(rows + i * pitch, blocks[1].shape[0]) for i in range(3)]
    if pitch > blocks[1].shape[0]:
        x[rows:] = jnp.zeros_like(x[rows:])
    for block, (first, count) in zip(blocks, spans):
        x[first : first + count] = block[:, :width]
    for c, w_ref in enumerate((w0_ref, w1_ref)):
        both = jnp.dot(x[...], w_ref[...], preferred_element_type=F32)
        gate = both[:, :ff]
        hid[:, c * ff : (c + 1) * ff] = (gate / (1.0 + jnp.exp(-gate)) * both[:, ff:]).astype(BF)
    scales = [weight_for(block[:, width:], expert, top) for block in blocks]
    tile = 1024
    for n in range(width // tile):
        s = slice(n * tile, (n + 1) * tile)
        out = jnp.dot(hid[:, :ff], d0_ref[:, s], preferred_element_type=F32)
        out = out + jnp.dot(hid[:, ff:], d1_ref[:, s], preferred_element_type=F32)
        for ref, scale, (first, count) in zip(outs, scales, spans):
            ref[:, s] = (out[first : first + count] * scale).astype(BF)


def run_expert(experts, blocks, weights, top):
    rows, wide = blocks[0].shape
    slots = blocks[1].shape[0]
    width = weights[0].shape[0]
    ff = weights[1].shape[0]
    pitch = -(-slots // 16) * 16
    total = rows + 3 * pitch
    return pl.pallas_call(
        functools.partial(expert_kernel, top, pitch),
        out_shape=[jax.ShapeDtypeStruct((block.shape[0], width), BF) for block in blocks],
        in_specs=whole_specs(8),
        out_specs=[pl.BlockSpec(memory_space=pltpu.VMEM)] * 4,
        scratch_shapes=[pltpu.VMEM((total, width), BF), pltpu.VMEM((total, 2 * ff), BF)],
        compiler_params=pltpu.CompilerParams(vmem_limit_bytes=14 << 20),
        cost_estimate=pl.CostEstimate(
            flops=12 * total * width * ff, bytes_accessed=4 * total * width, transcendentals=2 * total * ff
        ),
    )(experts, *blocks, *weights)


def put_back_kernel(top, slots, n_more, experts_ref, own_ref, block_ref, *refs):
    got, more, out_ref = refs[:3], refs[3 : 3 + n_more], refs[3 + n_more]
    width = own_ref.shape[1]
    place = one_hot(block_ref[:, width:], experts_ref, top, slots)
    rows = jnp.concatenate([ref[...] for ref in got], axis=0)
    total = own_ref[...].astype(F32) + jnp.dot(place, rows, preferred_element_type=F32)
    for ref in more:
        total = total + ref[...].astype(F32)
    out_ref[...] = total.astype(BF)


def put_back(experts, own, block, got, more, top):
    rows, width = own.shape
    slots = got[0].shape[0]
    return pl.pallas_call(
        functools.partial(put_back_kernel, top, slots, len(more)),
        out_shape=jax.ShapeDtypeStruct((rows, width), BF),
        in_specs=whole_specs(5 + len(more)),
        out_specs=pl.BlockSpec(memory_space=pltpu.VMEM),
        compiler_params=pltpu.CompilerParams(vmem_limit_bytes=12 << 20),
        cost_estimate=pl.CostEstimate(
            flops=6 * slots * rows * width, bytes_accessed=(8 + 2 * len(more)) * rows * width, transcendentals=0
        ),
    )(experts, own, block, *got, *more)


def on_device(tokens, expert_ids, route_weights, gate_proj, up_proj, down_proj):
    rows, width = tokens.shape
    top = expert_ids.shape[1]
    n_ep = lax.axis_size("ep")
    ring = n_ep // 4
    cap = max(2, min(rows, rows * top * 5 // (4 * n_ep)))
    slots = -(-cap // 8) * 8
    me = lax.axis_index("ep").astype(jnp.int32)

    def swap(x):
        return lax.ppermute(x, "etp", [(0, 1), (1, 0)])

    def hop_z(x):
        return lax.ppermute(x, "ep", [(i, (i + 4) % n_ep) for i in range(n_ep)])

    def spread(arrays):
        return [
            lax.ppermute(x, "ep", [(i, i ^ flip) for i in range(n_ep)]) for flip, x in zip((1, 2, 3), arrays)
        ]

    def after(x, *others):
        return lax.optimization_barrier((x, *others))[0]

    experts = jnp.stack([me, me ^ 1, me ^ 2, me ^ 3])
    block = prepare(expert_ids, route_weights, tokens)
    half = (gate_proj[0], up_proj[0], down_proj[0])
    other = []

    levels, given, results, weights = [block], [], [], []

    def compute(k):
        if not weights:
            other.extend(swap(x) for x in after(half, levels[1]))
            weights.extend([*stage(*after(half, levels[1])), *stage(*other)])
        mine = after(given[k], results[-1][0]) if results else given[k]
        results.append(run_expert(experts, [levels[k], *mine], weights, top))

    for k in range(ring):
        z = levels[k]
        if k:
            z = levels[k] = after(z, given[k - 1])
        if k > 1:
            compute(k - 2)
        if k + 1 < ring:
            levels.append(hop_z(z))
        given.append(spread(select(experts, z, top, slots)))

    carry = None
    returned = None
    for k in [*range(1, ring), 0]:
        while len(results) < min(ring, k + 2):
            compute(len(results))
        pz, *out = results[k]
        returned = spread(out)
        carry = put_back(experts, pz, levels[k], returned, [] if carry is None else [hop_z(carry)], top)
    return carry
def solution(mesh):
    in_specs = (
        P(("groups", "ep", "etp"), None),
        P(("groups", "ep", "etp"), None),
        P(("groups", "ep", "etp"), None),
        P("ep", None, "etp"),
        P("ep", None, "etp"),
        P("ep", "etp", None),
    )
    out_specs = P(("groups", "ep", "etp"), None)
    return jax.shard_map(
        on_device, mesh=mesh, in_specs=in_specs, out_specs=out_specs, check_vma=False
    )
```
